256 devices in a mesh: row: 16 (over y, z_hi), col: 16 (over z_lo, x, core).
Axes of the slice: x: 4, y: 4, z: 8 (z_hi: 4, z_lo: 2; z = z_hi * 2 + z_lo), core: 2. Of those that a mesh axis runs over, the one named last changes fastest.
Arguments:
- fock_matrix: bfloat16 [8192, 8192], P('row', 'col'), may hold values from -0.0625 to 0.0625
- intersection: bfloat16 [8192, 8192], P('row', 'col'), may hold values from -0.0625 to 0.0625
- density_panel: bfloat16 [1024, 8192], P('col', 'row'), may hold values from -6 to 6
- fock_mask: int32 [16, 16], P('row', 'col'), may hold values from 0 to 1, as said below
- intersection_mask: int32 [16, 16], P('row', 'col'), may hold values from 0 to 1, as said below
- density_mask: int32 [2, 16], P(None, 'row'), may hold values 0 or 1
Outputs:
- sigma_window: float32 [8192, 8192], P('row', 'col')
The draws below stay inside these ranges and needn't reach their ends.
Inputs may be any that keep to these rules, and one draw needn't show every extreme that they name: `fock_mask`: each entry flags one 512 x 512 tile; the diagonal tiles are always present. `intersection_mask`: each entry flags one 512 x 512 tile; the diagonal tiles are always present.
All inputs are finite; a program needn't handle non-finite values. No bound on the sum of `density_mask` on one device may be relied on, other than what follows from the above.
Results may differ from the reference program's by a relative error of at most 0.0029.
Values may be sent and summed in bfloat16 or wider, within the bound.
A program may use at most 64 MiB of HBM per device.

```python
import jax
import jax.numpy as jnp
from jax import lax

KW = 1024
KT = 2
NT = 16
M = 8192


def banded_tiles(key, spread_floor):
    scores = jax.random.randint(key, (NT, NT), 0, 1000)
    row_ids = lax.broadcasted_iota(jnp.int32, (NT, NT), 0)
    col_ids = lax.broadcasted_iota(jnp.int32, (NT, NT), 1)
    distance = jnp.abs(row_ids - col_ids)
    limits = jnp.maximum(1000 - 2000 * distance // NT, spread_floor)
    return (scores < limits).astype(jnp.int32)


def draw_fock_mask(key, part):
    key = jax.random.fold_in(key, 5)
    return banded_tiles(key, 150)


def draw_intersection_mask(key, part):
    key = jax.random.fold_in(key, 9)
    return banded_tiles(key, 100)


def set_ends(entries, rng, low, high):
    place = [jax.random.randint(jax.random.fold_in(rng, axis), (), 0, length) for axis, length in enumerate(entries.shape)]
    longest = entries.shape.index(max(entries.shape))
    neighbour = place[:longest] + [(place[longest] + 1) % entries.shape[longest]] + place[longest + 1:]
    return entries.at[tuple(place)].set(low).at[tuple(neighbour)].set(high)


def shard_levels(stream_key, extent, pieces, smallest, top_value):
    gain, own = 1.0, jax.random.fold_in(stream_key, 6)
    for dim, shards_of in pieces:
        draws = jnp.exp(jax.random.uniform(jax.random.fold_in(own, dim), (shards_of,), jnp.float32, smallest / len(pieces), top_value / len(pieces)))
        gain = gain * jnp.repeat(draws, extent[dim] // shards_of).reshape([-1 if axis == dim else 1 for axis in range(len(extent))])
    return gain


def noise(stream_key, dims, spread, bound, cuts=(), held_as=jnp.bfloat16):
    factor_of = shard_levels(stream_key, dims, cuts, -0.22, 0.18) if cuts else 1.0
    result = jax.random.normal(stream_key, dims, jnp.float32) * spread * factor_of
    return jnp.minimum(jnp.maximum(result, -bound), bound).astype(held_as)


def setup_inputs(seed: int = 0) -> dict:
    arg_keys = jax.random.split(jax.random.key(seed), 7)
    fock_matrix = noise(arg_keys[0], (M, M), M ** -0.5, 0.0625, ((0, 16), (1, 16)))
    intersection = noise(arg_keys[1], (M, M), M ** -0.5, 0.0625, ((0, 16), (1, 16)))
    density_panel = noise(arg_keys[2], (KW, M), 1.0, 6.0, ((0, 16), (1, 16)))
    fock_mask = draw_fock_mask(jax.random.fold_in(arg_keys[6], 71), 0)
    intersection_mask = draw_intersection_mask(jax.random.fold_in(arg_keys[6], 71), 0)
    density_mask = set_ends((jax.random.randint(arg_keys[5], (KT, NT), 0, 5) < 3).astype(jnp.int32), jax.random.fold_in(arg_keys[5], 1), 0, 1)
    return {"fock_matrix": fock_matrix, "intersection": intersection, "density_panel": density_panel, "fock_mask": fock_mask, "intersection_mask": intersection_mask, "density_mask": density_mask}


def zero_masked(matrix, tile_mask):
    rows_t, cols_t = tile_mask.shape
    shaped = matrix.reshape(rows_t, matrix.shape[0] // rows_t, cols_t, matrix.shape[1] // cols_t)
    factor_keep = tile_mask.astype(matrix.dtype)[:, None, :, None]
    return (shaped * factor_keep).reshape(matrix.shape)


def reference(fock_matrix, intersection, density_panel, fock_mask, intersection_mask, density_mask):
    fock_tiles = zero_masked(fock_matrix, fock_mask)
    intersection_tiles = zero_masked(intersection, intersection_mask)
    density_tiles = zero_masked(density_panel, density_mask)
    right_product = jnp.dot(density_tiles, intersection_tiles, preferred_element_type=jnp.float32).astype(jnp.bfloat16)
    left_product = jnp.dot(density_tiles, fock_tiles, preferred_element_type=jnp.float32).astype(jnp.bfloat16)
    first_term = jnp.dot(fock_tiles[:, :KW], right_product, preferred_element_type=jnp.float32)
    second_term = jnp.dot(intersection_tiles[:, :KW], left_product, preferred_element_type=jnp.float32)
    return first_term - second_term
```

```python
import jax
import jax.numpy as jnp
from jax import lax
from jax.experimental import pallas as pl
from jax.experimental.pallas import tpu as pltpu
from jax.sharding import PartitionSpec as P

MESH = pl.DeviceIdType.MESH
NC = 4
LN = 128
QR = 256
ZR = 64
SR = 16
TOP = 32000.0
TINY = 2.0**-100


def encode(value):
    amax = jnp.max(jnp.abs(value), axis=0, keepdims=True)
    t = jnp.ceil(jnp.log2(jnp.maximum(amax, TINY)))
    q = jnp.round(value * (jnp.exp2(-t) * TOP)).astype(jnp.int32).astype(jnp.int16)
    return q, t


def decode(q, t):
    return q.astype(jnp.int32).astype(jnp.float32) * (jnp.exp2(t) * (1.0 / TOP))


def kernel(
    f_ref, s_ref, d_ref, fm_ref, sm_ref, dm_ref, out_ref,
    w, dg, ys, yr, pf, zs, zr, yq, qg, strips, rn,
    d_ss, d_rs, c_ss, c_rs, t_ss, t_rs, t0_ss, t0_rs,
    ys_ss, ys_rs, zs_ss, zs_rs, za_ss, za_rs, ya_ss, ya_rs,
):
    row, col = lax.axis_index("row"), lax.axis_index("col")
    y, zh = row // 4, row % 4
    zl, x, core = col // 8, (col // 2) % 4, col % 2
    p = zl * 4 + x

    def group_peer(o):
        return (row, ((zl + o // 4) % 2) * 8 + ((x + o % 4) % 4) * 2 + core)

    def chip_of(o):
        return ((zl + o // 4) % 2) * 4 + (x + o % 4) % 4

    def y_peer(d):
        return (((y + d) % 4) * 4 + zh, col)

    def z_peer(d):
        return (y * 4 + (zh + d) % 4, col)

    core_peer = (row, zl * 8 + x * 2 + 1 - core)
    up, down = y_peer(1), y_peer(3)

    started = []

    def copy(src, dst, ss, rs, to):
        return pltpu.make_async_remote_copy(
            src_ref=src, dst_ref=dst, send_sem=ss, recv_sem=rs, device_id=to, device_id_type=MESH
        )

    def send(src, dst, ss, rs, to):
        c = copy(src, dst, ss, rs, to)
        c.start()
        started.append(c)
        return c

    barrier = pltpu.get_barrier_semaphore()
    partners = [group_peer(o) for o in range(1, 8)]
    partners += [core_peer, up, down] + [z_peer(d) for d in (1, 2, 3)]
    for to in partners:
        pl.semaphore_signal(barrier, inc=1, device_id=to, device_id_type=MESH)

    dmask = dm_ref[zl, 0].astype(jnp.float32)
    for d in range(4):
        rows = d_ref[(y + 2 + d) % 4]
        dg[d, p, core] = (rows.astype(jnp.float32) * dmask).astype(jnp.bfloat16)
    fmask = fm_ref[0, 0].astype(jnp.float32)
    smask = sm_ref[0, 0].astype(jnp.float32)
    pl.semaphore_wait(barrier, len(partners))

    d0 = [send(dg.at[0, p, core], dg.at[0, p, core], d_ss.at[0, o], d_rs.at[0, o], group_peer(o)) for o in range(1, 8)]
    d1 = [
        send(dg.at[pl.ds(1, 3), p, core], dg.at[pl.ds(1, 3), p, core], d_ss.at[1, o], d_rs.at[1, o], group_peer(o))
        for o in range(1, 8)
    ]

    s_all = (s_ref[...].astype(jnp.float32) * smask).astype(jnp.bfloat16)
    f_all = (f_ref[...].astype(jnp.float32) * fmask).astype(jnp.bfloat16)
    for n in range(NC):
        w[n, :, :LN] = s_all[:, n * LN : (n + 1) * LN]
        w[n, :, LN:] = f_all[:, n * LN : (n + 1) * LN]

    @pl.when(p == 0)
    def _():
        for i in range(4):
            strips[core, i] = f_all[i * 128 : (i + 1) * 128]
            strips[core, 4 + i] = s_all[i * 128 : (i + 1) * 128]
        for i in range(1, 8):
            copy(strips.at[core, i], strips.at[core, i], t0_ss.at[i], t0_rs, (row, 2 * i + core)).start()

    def strips_spread():
        @pl.when(p != 0)
        def _():
            copy(strips.at[core, p], strips.at[core, p], t0_ss.at[0], t0_rs, core_peer).wait_recv()

        for o in range(1, 8):
            @pl.when(chip_of(o) != 0)
            def _():
                copy(strips.at[core, p], strips.at[core, p], t_ss.at[o], t_rs.at[o], group_peer(o)).start()

    def strips_swap():
        @pl.when(p != 0)
        def _():
            for o in range(1, 8):
                copy(strips.at[core, p], strips.at[core, p], t_ss.at[o], t_rs.at[o], core_peer).wait_recv()

        return send(strips.at[core], strips.at[core], c_ss.at[2], c_rs.at[2], core_peer)

    def product(d, n):
        return jnp.dot(dg[d].reshape(QR, 512), w[n], preferred_element_type=jnp.float32)

    y_sent = {}

    def send_y(n, i, value):
        q, t = encode(value)
        ys[n, i, :QR] = q
        ys[n, i, QR:] = jnp.broadcast_to(t, (SR, LN)).astype(jnp.int32).astype(jnp.int16)
        y_sent[n, i] = send(ys.at[n, i], yr.at[n, i], ys_ss.at[n, i], ys_rs.at[n, i], down if i % 2 else up)

    def recv_y(n, i):
        y_sent[n, i].wait_recv()
        t = yr[n, i, QR:].astype(jnp.int32).astype(jnp.float32)[:1]
        return decode(yr[n, i, :QR], t)

    def a_opposite(n):
        v = product(0, n)
        send_y(n, 0, v[:, :LN])
        send_y(n, 1, v[:, LN:])

    def a_rest(n):
        v = product(3, n)
        send_y(n, 2, v[:, LN:])
        pf[n, 0] = v[:, :LN]
        v = product(1, n)
        send_y(n, 3, v[:, :LN])
        pf[n, 1] = v[:, LN:]

    def b(n):
        send_y(n, 4, pf[n, 0] + recv_y(n, 0))
        send_y(n, 5, pf[n, 1] + recv_y(n, 1))

    z_sent = {}

    def c(n):
        v = product(2, n)
        left = v[:, LN:] + recv_y(n, 2)
        right = v[:, :LN] + recv_y(n, 3)
        right = right + recv_y(n, 4)
        left = left + recv_y(n, 5)
        yq[n, 0] = right.reshape(4, ZR, LN)
        yq[n, 1] = left.reshape(4, ZR, LN)
        for d in (2, 1, 3):
            to = (zh + d) % 4
            q0, t0 = encode(yq[n, 0, to])
            q1, t1 = encode(yq[n, 1, to])
            zs[n, d, :ZR] = q0
            zs[n, d, ZR : 2 * ZR] = q1
            t = jnp.concatenate([jnp.broadcast_to(t0, (8, LN)), jnp.broadcast_to(t1, (8, LN))], axis=0)
            zs[n, d, 2 * ZR :] = t.astype(jnp.int32).astype(jnp.int16)
            z_sent[n, d] = send(zs.at[n, d], zr.at[n, d], zs_ss.at[n, d], zs_rs.at[n, d], z_peer(d))

    za_sent = {}

    def e(n):
        right, left = yq[n, 0, zh], yq[n, 1, zh]
        for d in (1, 3, 2):
            z_sent[n, d].wait_recv()
            t = zr[n, d, 2 * ZR :].astype(jnp.int32).astype(jnp.float32)
            right = right + decode(zr[n, d, :ZR], t[:1])
            left = left + decode(zr[n, d, ZR : 2 * ZR], t[8:9])
        qg[n, y, 0, zh] = right.astype(jnp.bfloat16)
        qg[n, y, 1, zh] = left.astype(jnp.bfloat16)
        mine = qg.at[n, y, :, zh]
        for d in (2, 1, 3):
            za_sent[n, d] = send(mine, mine, za_ss.at[n, d], za_rs.at[n, d], z_peer(d))

    ya_sent = {}

    def g(n):
        for d in (1, 3, 2):
            za_sent[n, d].wait_recv()
        mine = qg.at[n, y]
        ya_sent[n, 0] = send(mine, mine, ya_ss.at[n, 0], ya_rs.at[n, 0], up)
        ya_sent[n, 1] = send(mine, mine, ya_ss.at[n, 1], ya_rs.at[n, 1], down)

    def h(n):
        ya_sent[n, 0].wait_recv()
        part = qg.at[n, (y + 3) % 4, 0]
        ya_sent[n, 2] = send(part, part, ya_ss.at[n, 2], ya_rs.at[n, 2], up)
        ya_sent[n, 1].wait_recv()
        part = qg.at[n, (y + 1) % 4, 1]
        ya_sent[n, 3] = send(part, part, ya_ss.at[n, 3], ya_rs.at[n, 3], down)

    def k(n):
        ya_sent[n, 2].wait_recv()
        ya_sent[n, 3].wait_recv()
        for m in range(2):
            for q in range(4):
                for cc in range(16):
                    at = cc * 64 + q * 16
                    rn[m, at : at + 16] = qg[n, q, m, cc // 4, (cc % 4) * 16 : (cc % 4) * 16 + 16]
        total = None
        for m in range(2):
            for half in range(2):
                lhs = strips[half, 4 * m : 4 * m + 4].reshape(512, 512)
                part = jnp.dot(lhs, rn[m, half * 512 : (half + 1) * 512], preferred_element_type=jnp.float32)
                total = part if total is None else (total + part if m == 0 else total - part)
        out_ref[:, n * LN : (n + 1) * LN] = total

    for cp in d0:
        cp.wait_recv()
    swap0 = send(dg.at[0, :, core], dg.at[0, :, core], c_ss.at[0], c_rs.at[0], core_peer)
    swap0.wait_recv()
    a_opposite(0)
    a_opposite(1)
    for cp in d1:
        cp.wait_recv()
    tail = pl.ds(1, 3)
    swap1 = send(dg.at[tail, :, core], dg.at[tail, :, core], c_ss.at[1], c_rs.at[1], core_peer)
    swap1.wait_recv()
    a_rest(0)
    b(0)
    a_opposite(2)
    a_rest(1)
    b(1)
    strips_spread()
    c(0)
    a_opposite(3)
    a_rest(2)
    b(2)
    c(1)
    e(0)
    a_rest(3)
    b(3)
    c(2)
    e(1)
    g(0)
    c(3)
    e(2)
    g(1)
    h(0)
    swap2 = strips_swap()
    e(3)
    g(2)
    h(1)
    swap2.wait_recv()
    k(0)
    g(3)
    h(2)
    k(1)
    h(3)
    k(2)
    k(3)

    for cp in started:
        cp.wait_send()

    @pl.when(p == 0)
    def _():
        for i in range(1, 8):
            copy(strips.at[core, i], strips.at[core, i], t0_ss.at[i], t0_rs, core_peer).wait_send()

    for o in range(1, 8):
        @pl.when(chip_of(o) != 0)
        def _():
            copy(strips.at[core, p], strips.at[core, p], t_ss.at[o], t_rs.at[o], core_peer).wait_send()


def per_device(fock_matrix, intersection, density_panel, fock_mask, intersection_mask, density_mask):
    vmem = pl.BlockSpec(memory_space=pltpu.VMEM)
    smem = pl.BlockSpec(memory_space=pltpu.SMEM)
    dma = pltpu.SemaphoreType.DMA
    return pl.pallas_call(
        kernel,
        out_shape=jax.ShapeDtypeStruct((512, 512), jnp.float32),
        in_specs=[vmem, vmem, vmem, smem, smem, smem],
        out_specs=vmem,
        scratch_shapes=[
            pltpu.VMEM((NC, 512, 2 * LN), jnp.bfloat16),
            pltpu.VMEM((4, 8, 2, 16, 512), jnp.bfloat16),
            pltpu.VMEM((NC, 6, QR + SR, LN), jnp.int16),
            pltpu.VMEM((NC, 6, QR + SR, LN), jnp.int16),
            pltpu.VMEM((NC, 2, QR, LN), jnp.float32),
            pltpu.VMEM((NC, 4, 2 * ZR + SR, LN), jnp.int16),
            pltpu.VMEM((NC, 4, 2 * ZR + SR, LN), jnp.int16),
            pltpu.VMEM((NC, 2, 4, ZR, LN), jnp.float32),
            pltpu.VMEM((NC, 4, 2, 4, ZR, LN), jnp.bfloat16),
            pltpu.VMEM((2, 8, 128, 512), jnp.bfloat16),
            pltpu.VMEM((2, 1024, LN), jnp.bfloat16),
            dma((2, 8)), dma((2, 8)), dma((3,)), dma((3,)), dma((8,)), dma((8,)), dma((8,)), dma(()),
            dma((NC, 6)), dma((NC, 6)), dma((NC, 4)), dma((NC, 4)), dma((NC, 4)), dma((NC, 4)),
            dma((NC, 4)), dma((NC, 4)),
        ],
        compiler_params=pltpu.CompilerParams(
            collective_id=0, has_side_effects=True, vmem_limit_bytes=40 * 2**20
        ),
        cost_estimate=pl.CostEstimate(flops=2 * 2**30, bytes_accessed=3 * 2**20, transcendentals=0),
    )(
        fock_matrix,
        intersection,
        density_panel.reshape(4, 16, 512),
        fock_mask,
        intersection_mask,
        density_mask,
    )


def solution(mesh):
    placed = (
        P("row", "col"),
        P("row", "col"),
        P("col", "row"),
        P("row", "col"),
        P("row", "col"),
        P(None, "row"),
    )
    return jax.shard_map(
        per_device, mesh=mesh, in_specs=placed, out_specs=P("row", "col"), check_vma=False
    )
```

```python
import jax
import jax.numpy as jnp
from jax import lax
from jax.experimental import pallas as pl
from jax.experimental.pallas import tpu as pltpu
from jax.sharding import PartitionSpec as P

MESH = pl.DeviceIdType.MESH
NC = 4
LN = 128
SR = 16
HR = 128
HZ = 32
TOP = 32000.0
TINY = 2.0**-100
JOBS = ((0, (0, 1)), (1, (0, 1)), (2, (0, 1)), (3, (0, 1)))
NJ = len(JOBS)
ORDER = (
    "S0", "D.0", "a.0", "a.1", "D.1", "r.0", "r.1", "b.0", "a.2", "b.1", "r.2", "c.0", "a.3", "b.2",
    "r.3", "c.1", "S1", "e.0", "b.3", "c.2", "e.1", "g.0", "S2", "c.3", "e.2", "h.0", "g.1", "e.3",
    "h.1", "g.2", "S3", "h.2", "g.3", "S4", "k.0", "k.1", "h.3", "k.2", "k.3",
)


def encode(value):
    amax = jnp.max(jnp.abs(value), axis=0, keepdims=True)
    t = jnp.ceil(jnp.log2(jnp.maximum(amax, TINY)))
    q = jnp.round(value * (jnp.exp2(-t) * TOP)).astype(jnp.int32).astype(jnp.int16)
    return q, t


def decode(q, t):
    return q.astype(jnp.int32).astype(jnp.float32) * (jnp.exp2(t) * (1.0 / TOP))


def kernel(
    f_hbm, s_hbm, d_hbm, fm_hbm, sm_hbm, dm_hbm, out_ref,
    f_ref, s_ref, d_ref, fm_ref, sm_ref, dm_ref, in_sem,
    w, dg, ys, yr, pf, zs, zr, yq, qg, strips, rn,
    d_ss, d_rs, c_ss, c_rs, t_ss, t_rs, t0_ss, t0_rs,
    ys_ss, ys_rs, zs_ss, zs_rs, za_ss, za_rs, ya_ss, ya_rs,
):
    row, col = lax.axis_index("row"), lax.axis_index("col")
    y, zh = row // 4, row % 4
    zl, x, core = col // 8, (col // 2) % 4, col % 2
    p = zl * 4 + x

    def group_peer(o):
        return (row, ((zl + o // 4) % 2) * 8 + ((x + o % 4) % 4) * 2 + core)

    def chip_of(o):
        return ((zl + o // 4) % 2) * 4 + (x + o % 4) % 4

    def y_peer(d):
        return (((y + d) % 4) * 4 + zh, col)

    def z_peer(d):
        return (y * 4 + (zh + d) % 4, col)

    core_peer = (row, zl * 8 + x * 2 + 1 - core)
    up, down = y_peer(1), y_peer(3)

    started = []

    def copy(src, dst, ss, rs, to):
        return pltpu.make_async_remote_copy(
            src_ref=src, dst_ref=dst, send_sem=ss, recv_sem=rs, device_id=to, device_id_type=MESH
        )

    def send(src, dst, ss, rs, to):
        c = copy(src, dst, ss, rs, to)
        c.start()
        started.append(c)
        return c

    barrier = pltpu.get_barrier_semaphore()
    partners = [z_peer(d) for d in (2, 1, 3)] + [group_peer(o) for o in range(1, 8)]
    partners += [core_peer, up, down]
    for to in partners:
        pl.semaphore_signal(barrier, inc=1, device_id=to, device_id_type=MESH)

    ins = [
        pltpu.make_async_copy(src, dst, in_sem.at[i])
        for i, (src, dst) in enumerate(
            ((d_hbm, d_ref), (dm_hbm, dm_ref), (fm_hbm, fm_ref), (sm_hbm, sm_ref), (f_hbm, f_ref), (s_hbm, s_ref))
        )
    ]
    for cp in ins:
        cp.start()
    for cp in ins[:2]:
        cp.wait()
    dmask = dm_ref[0, zl].astype(jnp.float32)
    for d in range(4):
        rows = d_ref[(y + 2 + d) % 4]
        dg[d, p, core] = (rows.astype(jnp.float32) * dmask).astype(jnp.bfloat16)
    for cp in ins[2:]:
        cp.wait()
    fmask = fm_ref[0, 0].astype(jnp.float32)
    smask = sm_ref[0, 0].astype(jnp.float32)
    pl.semaphore_wait(barrier, len(partners))

    head, tail = pl.ds(0, 1), pl.ds(1, 3)
    d_sent = [
        [
            send(dg.at[part, p, core], dg.at[part, p, core], d_ss.at[i, o], d_rs.at[i, o], group_peer(o))
            for o in range(1, 8)
        ]
        for i, part in enumerate((head, tail))
    ]

    s_all = (s_ref[...].astype(jnp.float32) * smask).astype(jnp.bfloat16)
    f_all = (f_ref[...].astype(jnp.float32) * fmask).astype(jnp.bfloat16)
    for n in range(NC):
        w[n, :, :LN] = s_all[:, n * LN : (n + 1) * LN]
        w[n, :, LN:] = f_all[:, n * LN : (n + 1) * LN]

    @pl.when(p == 0)
    def _():
        for i in range(4):
            strips[core, i] = f_all[i * 128 : (i + 1) * 128]
            strips[core, 4 + i] = s_all[i * 128 : (i + 1) * 128]

    def swap_density(i):
        part = (head, tail)[i]
        for cp in d_sent[i]:
            cp.wait_recv()
        cp = send(dg.at[part, :, core], dg.at[part, :, core], c_ss.at[i], c_rs.at[i], core_peer)
        cp.wait_recv()

    def strip(i):
        return strips.at[core, i]

    def strips_0(_):
        @pl.when(p == 0)
        def _():
            for i in range(1, 8):
                copy(strip(i), strip(i), t0_ss.at[i], t0_rs, (row, 2 * i + core)).start()

    def strips_1(_):
        @pl.when(p != 0)
        def _():
            copy(strip(p), strip(p), t0_ss.at[0], t0_rs, core_peer).wait_recv()

        for o in (4, 2, 1, 3):
            @pl.when(chip_of(o) != 0)
            def _():
                copy(strip(p), strip(p), t_ss.at[o], t_rs.at[o], group_peer(o)).start()

    other = (1 - zl) * 4 + x

    def strips_2(_):
        @pl.when(p != 0)
        def _():
            copy(strip(other), strip(other), t_ss.at[4], t_rs.at[4], core_peer).wait_recv()

        for o in (2, 1, 3):
            @pl.when(chip_of(o) != 0)
            def _():
                copy(strip(other), strip(other), t_ss.at[4 + o], t_rs.at[4 + o], group_peer(o)).start()

    swaps = []

    def strips_3(_):
        @pl.when(p != 0)
        def _():
            for o in (1, 2, 3, 5, 6, 7):
                copy(strip(p), strip(p), t_ss.at[o], t_rs.at[o], core_peer).wait_recv()

        swaps.append(send(strips.at[core], strips.at[core], c_ss.at[2], c_rs.at[2], core_peer))

    def strips_4(_):
        swaps[0].wait_recv()

    def product(d, j):
        n, hs = JOBS[j]
        rows = dg[d, 4 * hs[0] : 4 * hs[-1] + 4].reshape(HR * len(hs), 512)
        return jnp.dot(rows, w[n], preferred_element_type=jnp.float32)

    y_sent = {}

    def send_y(j, i, value):
        q, t = encode(value)
        m = value.shape[0]
        ys[j, i, :m] = q
        ys[j, i, m : m + SR] = jnp.broadcast_to(t, (SR, LN)).astype(jnp.int32).astype(jnp.int16)
        part = pl.ds(0, m + SR)
        y_sent[j, i] = send(
            ys.at[j, i, part], yr.at[j, i, part], ys_ss.at[j, i], ys_rs.at[j, i], down if i % 2 else up
        )

    def recv_y(j, i):
        m = HR * len(JOBS[j][1])
        y_sent[j, i].wait_recv()
        t = yr[j, i, m : m + SR].astype(jnp.int32).astype(jnp.float32)[:1]
        return decode(yr[j, i, :m], t)

    def a(j):
        v = product(0, j)
        send_y(j, 0, v[:, :LN])
        send_y(j, 1, v[:, LN:])

    def r(j):
        m = HR * len(JOBS[j][1])
        v = product(3, j)
        send_y(j, 2, v[:, LN:])
        pf[j, 0, :m] = v[:, :LN]
        v = product(1, j)
        send_y(j, 3, v[:, :LN])
        pf[j, 1, :m] = v[:, LN:]

    def b(j):
        m = HR * len(JOBS[j][1])
        send_y(j, 4, pf[j, 0, :m] + recv_y(j, 0))
        send_y(j, 5, pf[j, 1, :m] + recv_y(j, 1))

    z_sent = {}

    def c(j):
        nh = len(JOBS[j][1])
        v = product(2, j)
        left = v[:, LN:] + recv_y(j, 2)
        right = v[:, :LN] + recv_y(j, 3)
        right = right + recv_y(j, 4)
        left = left + recv_y(j, 5)
        yq[j, 0, :nh] = right.reshape(nh, 4, HZ, LN)
        yq[j, 1, :nh] = left.reshape(nh, 4, HZ, LN)
        m = HZ * nh
        part = pl.ds(0, 2 * m + SR)
        for d in (2, 1, 3):
            to = (zh + d) % 4
            q0, t0 = encode(yq[j, 0, :nh, to].reshape(m, LN))
            q1, t1 = encode(yq[j, 1, :nh, to].reshape(m, LN))
            zs[j, d, :m] = q0
            zs[j, d, m : 2 * m] = q1
            t = jnp.concatenate([jnp.broadcast_to(t0, (8, LN)), jnp.broadcast_to(t1, (8, LN))], axis=0)
            zs[j, d, 2 * m : 2 * m + SR] = t.astype(jnp.int32).astype(jnp.int16)
            z_sent[j, d] = send(zs.at[j, d, part], zr.at[j, d, part], zs_ss.at[j, d], zs_rs.at[j, d], z_peer(d))

    za_sent = {}

    def e(j):
        n, hs = JOBS[j]
        nh = len(hs)
        m = HZ * nh
        right = yq[j, 0, :nh, zh].reshape(m, LN)
        left = yq[j, 1, :nh, zh].reshape(m, LN)
        for d in (1, 3, 2):
            z_sent[j, d].wait_recv()
            t = zr[j, d, 2 * m : 2 * m + SR].astype(jnp.int32).astype(jnp.float32)
            right = right + decode(zr[j, d, :m], t[:1])
            left = left + decode(zr[j, d, m : 2 * m], t[8:9])
        rows = slice(hs[0], hs[0] + nh)
        qg[n, y, 0, rows, zh] = right.astype(jnp.bfloat16).reshape(nh, HZ, LN)
        qg[n, y, 1, rows, zh] = left.astype(jnp.bfloat16).reshape(nh, HZ, LN)
        mine = qg.at[n, y, :, pl.ds(hs[0], nh), zh]
        for d in (2, 1, 3):
            za_sent[j, d] = send(mine, mine, za_ss.at[j, d], za_rs.at[j, d], z_peer(d))

    ya_sent = {}

    def g(j):
        n, hs = JOBS[j]
        for d in (1, 3, 2):
            za_sent[j, d].wait_recv()
        rows = pl.ds(hs[0], len(hs))
        for i, (m, to) in enumerate(((0, up), (1, down), (1, up), (0, down))):
            mine = qg.at[n, y, m, rows]
            ya_sent[j, i] = send(mine, mine, ya_ss.at[j, i], ya_rs.at[j, i], to)

    def h(j):
        n, hs = JOBS[j]
        rows = pl.ds(hs[0], len(hs))
        ya_sent[j, 0].wait_recv()
        part = qg.at[n, (y + 3) % 4, 0, rows]
        ya_sent[j, 4] = send(part, part, ya_ss.at[j, 4], ya_rs.at[j, 4], up)
        ya_sent[j, 1].wait_recv()
        part = qg.at[n, (y + 1) % 4, 1, rows]
        ya_sent[j, 5] = send(part, part, ya_ss.at[j, 5], ya_rs.at[j, 5], down)

    def k(j):
        n, hs = JOBS[j]
        for i in (2, 3, 4, 5):
            ya_sent[j, i].wait_recv()
        at = slice(n * LN, (n + 1) * LN)
        total = None
        for half in hs:
            for m in range(2):
                for q in range(4):
                    for cc in range(8):
                        to = cc * 64 + q * 16
                        rn[m, to : to + 16] = qg[n, q, m, half, cc // 2, (cc % 2) * 16 : (cc % 2) * 16 + 16]
            for m in range(2):
                lhs = strips[half, 4 * m : 4 * m + 4].reshape(512, 512)
                part = jnp.dot(lhs, rn[m], preferred_element_type=jnp.float32)
                total = part if total is None else (total + part if m == 0 else total - part)
        out_ref[:, at] = total if hs[0] == 0 else out_ref[:, at] + total

    steps = {"D": swap_density, "S0": strips_0, "S1": strips_1, "S2": strips_2, "S3": strips_3, "S4": strips_4}
    steps.update(a=a, r=r, b=b, c=c, e=e, g=g, h=h, k=k)
    for word in ORDER:
        name, _, j = word.partition(".")
        steps[name](int(j or 0))

    for cp in started:
        cp.wait_send()

    @pl.when(p == 0)
    def _():
        for i in range(1, 8):
            copy(strip(i), strip(i), t0_ss.at[i], t0_rs, core_peer).wait_send()

    for o in range(1, 8):
        @pl.when(chip_of(o % 4 if o != 4 else 4) != 0)
        def _():
            copy(strip(p), strip(p), t_ss.at[o], t_rs.at[o], core_peer).wait_send()


def per_device(fock_matrix, intersection, density_panel, fock_mask, intersection_mask, density_mask):
    vmem = pl.BlockSpec(memory_space=pltpu.VMEM)
    hbm = pl.BlockSpec(memory_space=pltpu.HBM)
    dma = pltpu.SemaphoreType.DMA
    bf16, f32, i16 = jnp.bfloat16, jnp.float32, jnp.int16
    return pl.pallas_call(
        kernel,
        out_shape=jax.ShapeDtypeStruct((512, 512), jnp.float32),
        in_specs=[hbm] * 6,
        out_specs=vmem,
        scratch_shapes=[
            pltpu.VMEM((512, 512), bf16),
            pltpu.VMEM((512, 512), bf16),
            pltpu.VMEM((4, 16, 512), bf16),
            pltpu.SMEM((1, 1), jnp.int32),
            pltpu.SMEM((1, 1), jnp.int32),
            pltpu.SMEM((1, 2), jnp.int32),
            dma((6,)),
            pltpu.VMEM((NC, 512, 2 * LN), bf16),
            pltpu.VMEM((4, 8, 2, 16, 512), bf16),
            pltpu.VMEM((NJ, 6, 2 * HR + SR, LN), i16),
            pltpu.VMEM((NJ, 6, 2 * HR + SR, LN), i16),
            pltpu.VMEM((NJ, 2, 2 * HR, LN), f32),
            pltpu.VMEM((NJ, 4, 4 * HZ + SR, LN), i16),
            pltpu.VMEM((NJ, 4, 4 * HZ + SR, LN), i16),
            pltpu.VMEM((NJ, 2, 2, 4, HZ, LN), f32),
            pltpu.VMEM((NC, 4, 2, 2, 4, HZ, LN), bf16),
            pltpu.VMEM((2, 8, 128, 512), bf16),
            pltpu.VMEM((2, 512, LN), bf16),
            dma((2, 8)), dma((2, 8)), dma((3,)), dma((3,)), dma((8,)), dma((8,)), dma((8,)), dma(()),
            dma((NJ, 6)), dma((NJ, 6)), dma((NJ, 4)), dma((NJ, 4)), dma((NJ, 4)), dma((NJ, 4)),
            dma((NJ, 6)), dma((NJ, 6)),
        ],
        compiler_params=pltpu.CompilerParams(
            collective_id=0, has_side_effects=True, vmem_limit_bytes=56 * 2**20
        ),
        cost_estimate=pl.CostEstimate(flops=2 * 2**30, bytes_accessed=3 * 2**20, transcendentals=0),
    )(
        fock_matrix,
        intersection,
        density_panel.reshape(4, 16, 512),
        fock_mask,
        intersection_mask,
        density_mask.T,
    )


def solution(mesh):
    placed = (
        P("row", "col"),
        P("row", "col"),
        P("col", "row"),
        P("row", "col"),
        P("row", "col"),
        P(None, "row"),
    )
    return jax.shard_map(
        per_device, mesh=mesh, in_specs=placed, out_specs=P("row", "col"), check_vma=False
    )
```

```python
import jax
import jax.numpy as jnp
from jax import lax
from jax.experimental import pallas as pl
from jax.experimental.pallas import tpu as pltpu
from jax.sharding import PartitionSpec as P

MESH = pl.DeviceIdType.MESH
NC = 4
LN = 128
SR = 16
HR = 128
HZ = 32
TOP = 32000.0
TINY = 2.0**-100
JOBS = ((0, (0, 1)), (1, (0, 1)), (2, (0, 1)), (3, (0, 1)))
NJ = len(JOBS)
ORDER = (
    "S0", "D.0", "a.0", "a.1", "D.1", "r.0", "r.1", "b.0", "a.2", "b.1", "r.2", "c.0", "a.3", "b.2",
    "r.3", "c.1", "b.3", "e.0", "S1", "c.2", "e.1", "c.3", "g.0", "S2", "e.2", "h.0", "g.1", "e.3",
    "h.1", "g.2", "S3", "h.2", "g.3", "S4", "k.0", "k.1", "h.3", "k.2", "k.3",
)


def encode(value):
    amax = jnp.max(jnp.abs(value), axis=0, keepdims=True)
    t = jnp.ceil(jnp.log2(jnp.maximum(amax, TINY)))
    q = jnp.round(value * (jnp.exp2(-t) * TOP)).astype(jnp.int32).astype(jnp.int16)
    return q, t


def decode(q, t):
    return q.astype(jnp.int32).astype(jnp.float32) * (jnp.exp2(t) * (1.0 / TOP))


def kernel(
    f_hbm, s_hbm, d_hbm, fm_hbm, sm_hbm, dm_hbm, out_ref,
    f_ref, s_ref, d_ref, fm_ref, sm_ref, dm_ref, in_sem, staged, out_sem,
    w, dg, ys, yr, pf, zs, zr, yq, qg, strips, rn,
    d_ss, d_rs, c_ss, c_rs, t_ss, t_rs, t0_ss, t0_rs,
    ys_ss, ys_rs, zs_ss, zs_rs, za_ss, za_rs, ya_ss, ya_rs,
):
    row, col = lax.axis_index("row"), lax.axis_index("col")
    y, zh = row // 4, row % 4
    zl, x, core = col // 8, (col // 2) % 4, col % 2
    p = zl * 4 + x

    def group_peer(o):
        return (row, ((zl + o // 4) % 2) * 8 + ((x + o % 4) % 4) * 2 + core)

    def chip_of(o):
        return ((zl + o // 4) % 2) * 4 + (x + o % 4) % 4

    def y_peer(d):
        return (((y + d) % 4) * 4 + zh, col)

    def z_peer(d):
        return (y * 4 + (zh + d) % 4, col)

    core_peer = (row, zl * 8 + x * 2 + 1 - core)
    up, down = y_peer(1), y_peer(3)

    started = []

    def copy(src, dst, ss, rs, to):
        return pltpu.make_async_remote_copy(
            src_ref=src, dst_ref=dst, send_sem=ss, recv_sem=rs, device_id=to, device_id_type=MESH
        )

    def send(src, dst, ss, rs, to):
        c = copy(src, dst, ss, rs, to)
        c.start()
        started.append(c)
        return c

    barrier = pltpu.get_barrier_semaphore()
    partners = [z_peer(d) for d in (2, 1, 3)] + [group_peer(o) for o in range(1, 8)]
    partners += [core_peer, up, down]
    for to in partners:
        pl.semaphore_signal(barrier, inc=1, device_id=to, device_id_type=MESH)

    ins = [
        pltpu.make_async_copy(src, dst, in_sem.at[i])
        for i, (src, dst) in enumerate(
            ((d_hbm, d_ref), (dm_hbm, dm_ref), (fm_hbm, fm_ref), (sm_hbm, sm_ref), (f_hbm, f_ref), (s_hbm, s_ref))
        )
    ]
    for cp in ins:
        cp.start()
    for cp in ins[:2]:
        cp.wait()
    dmask = dm_ref[0, zl].astype(jnp.float32)
    for d in range(4):
        rows = d_ref[(y + 2 + d) % 4]
        dg[d, p, core] = (rows.astype(jnp.float32) * dmask).astype(jnp.bfloat16)
    pl.semaphore_wait(barrier, len(partners))

    head, tail = pl.ds(0, 1), pl.ds(1, 3)
    d_sent = [
        [
            send(dg.at[part, p, core], dg.at[part, p, core], d_ss.at[i, o], d_rs.at[i, o], group_peer(o))
            for o in range(1, 8)
        ]
        for i, part in enumerate((head, tail))
    ]

    for cp in ins[2:]:
        cp.wait()
    fmask = fm_ref[0, 0].astype(jnp.float32)
    smask = sm_ref[0, 0].astype(jnp.float32)
    s_all = (s_ref[...].astype(jnp.float32) * smask).astype(jnp.bfloat16)
    f_all = (f_ref[...].astype(jnp.float32) * fmask).astype(jnp.bfloat16)
    for n in range(NC):
        w[n, :, :LN] = s_all[:, n * LN : (n + 1) * LN]
        w[n, :, LN:] = f_all[:, n * LN : (n + 1) * LN]

    @pl.when(p == 0)
    def _():
        for i in range(4):
            strips[core, i] = f_all[i * 128 : (i + 1) * 128]
            strips[core, 4 + i] = s_all[i * 128 : (i + 1) * 128]

    def swap_density(i):
        part = (head, tail)[i]
        for cp in d_sent[i]:
            cp.wait_recv()
        cp = send(dg.at[part, :, core], dg.at[part, :, core], c_ss.at[i], c_rs.at[i], core_peer)
        cp.wait_recv()

    def strip(i):
        return strips.at[core, i]

    def strips_0(_):
        @pl.when(p == 0)
        def _():
            for i in range(1, 8):
                copy(strip(i), strip(i), t0_ss.at[i], t0_rs, (row, 2 * i + core)).start()

    def strips_1(_):
        @pl.when(p != 0)
        def _():
            copy(strip(p), strip(p), t0_ss.at[0], t0_rs, core_peer).wait_recv()

        for o in (4, 2, 1, 3):
            @pl.when(chip_of(o) != 0)
            def _():
                copy(strip(p), strip(p), t_ss.at[o], t_rs.at[o], group_peer(o)).start()

    other = (1 - zl) * 4 + x

    def strips_2(_):
        @pl.when(p != 0)
        def _():
            copy(strip(other), strip(other), t_ss.at[4], t_rs.at[4], core_peer).wait_recv()

        for o in (2, 1, 3):
            @pl.when(chip_of(o) != 0)
            def _():
                copy(strip(other), strip(other), t_ss.at[4 + o], t_rs.at[4 + o], group_peer(o)).start()

    swaps = []
    outs = []

    def strips_3(_):
        @pl.when(p != 0)
        def _():
            for o in (1, 2, 3, 5, 6, 7):
                copy(strip(p), strip(p), t_ss.at[o], t_rs.at[o], core_peer).wait_recv()

        swaps.append(send(strips.at[core], strips.at[core], c_ss.at[2], c_rs.at[2], core_peer))

    def strips_4(_):
        swaps[0].wait_recv()

    def product(d, j):
        n, hs = JOBS[j]
        rows = dg[d, 4 * hs[0] : 4 * hs[-1] + 4].reshape(HR * len(hs), 512)
        return jnp.dot(rows, w[n], preferred_element_type=jnp.float32)

    y_sent = {}

    def send_y(j, i, value):
        q, t = encode(value)
        m = value.shape[0]
        ys[j, i, :m] = q
        ys[j, i, m : m + SR] = jnp.broadcast_to(t, (SR, LN)).astype(jnp.int32).astype(jnp.int16)
        part = pl.ds(0, m + SR)
        y_sent[j, i] = send(
            ys.at[j, i, part], yr.at[j, i, part], ys_ss.at[j, i], ys_rs.at[j, i], down if i % 2 else up
        )

    def recv_y(j, i):
        m = HR * len(JOBS[j][1])
        y_sent[j, i].wait_recv()
        t = yr[j, i, m : m + SR].astype(jnp.int32).astype(jnp.float32)[:1]
        return decode(yr[j, i, :m], t)

    def a(j):
        v = product(0, j)
        send_y(j, 0, v[:, :LN])
        send_y(j, 1, v[:, LN:])

    def r(j):
        m = HR * len(JOBS[j][1])
        v = product(3, j)
        send_y(j, 2, v[:, LN:])
        pf[j, 0, :m] = v[:, :LN]
        v = product(1, j)
        send_y(j, 3, v[:, :LN])
        pf[j, 1, :m] = v[:, LN:]

    def b(j):
        m = HR * len(JOBS[j][1])
        send_y(j, 4, pf[j, 0, :m] + recv_y(j, 0))
        send_y(j, 5, pf[j, 1, :m] + recv_y(j, 1))

    z_sent = {}

    def c(j):
        nh = len(JOBS[j][1])
        v = product(2, j)
        left = v[:, LN:] + recv_y(j, 2)
        right = v[:, :LN] + recv_y(j, 3)
        right = right + recv_y(j, 4)
        left = left + recv_y(j, 5)
        yq[j, 0, :nh] = right.reshape(nh, 4, HZ, LN)
        yq[j, 1, :nh] = left.reshape(nh, 4, HZ, LN)
        m = HZ * nh
        part = pl.ds(0, 2 * m + SR)
        for d in (2, 1, 3):
            to = (zh + d) % 4
            q0, t0 = encode(yq[j, 0, :nh, to].reshape(m, LN))
            q1, t1 = encode(yq[j, 1, :nh, to].reshape(m, LN))
            zs[j, d, :m] = q0
            zs[j, d, m : 2 * m] = q1
            t = jnp.concatenate([jnp.broadcast_to(t0, (8, LN)), jnp.broadcast_to(t1, (8, LN))], axis=0)
            zs[j, d, 2 * m : 2 * m + SR] = t.astype(jnp.int32).astype(jnp.int16)
            z_sent[j, d] = send(zs.at[j, d, part], zr.at[j, d, part], zs_ss.at[j, d], zs_rs.at[j, d], z_peer(d))

    za_sent = {}

    def e(j):
        n, hs = JOBS[j]
        nh = len(hs)
        m = HZ * nh
        right = yq[j, 0, :nh, zh].reshape(m, LN)
        left = yq[j, 1, :nh, zh].reshape(m, LN)
        for d in (1, 3, 2):
            z_sent[j, d].wait_recv()
            t = zr[j, d, 2 * m : 2 * m + SR].astype(jnp.int32).astype(jnp.float32)
            right = right + decode(zr[j, d, :m], t[:1])
            left = left + decode(zr[j, d, m : 2 * m], t[8:9])
        rows = slice(hs[0], hs[0] + nh)
        qg[n, y, 0, rows, zh] = right.astype(jnp.bfloat16).reshape(nh, HZ, LN)
        qg[n, y, 1, rows, zh] = left.astype(jnp.bfloat16).reshape(nh, HZ, LN)
        mine = qg.at[n, y, :, pl.ds(hs[0], nh), zh]
        for d in (2, 1, 3):
            za_sent[j, d] = send(mine, mine, za_ss.at[j, d], za_rs.at[j, d], z_peer(d))

    ya_sent = {}

    def g(j):
        n, hs = JOBS[j]
        for d in (1, 3, 2):
            za_sent[j, d].wait_recv()
        rows = pl.ds(hs[0], len(hs))
        for i, (m, to) in enumerate(((0, up), (1, down), (1, up), (0, down))):
            mine = qg.at[n, y, m, rows]
            ya_sent[j, i] = send(mine, mine, ya_ss.at[j, i], ya_rs.at[j, i], to)

    def h(j):
        n, hs = JOBS[j]
        rows = pl.ds(hs[0], len(hs))
        ya_sent[j, 0].wait_recv()
        part = qg.at[n, (y + 3) % 4, 0, rows]
        ya_sent[j, 4] = send(part, part, ya_ss.at[j, 4], ya_rs.at[j, 4], up)
        ya_sent[j, 1].wait_recv()
        part = qg.at[n, (y + 1) % 4, 1, rows]
        ya_sent[j, 5] = send(part, part, ya_ss.at[j, 5], ya_rs.at[j, 5], down)

    def k(j):
        n, hs = JOBS[j]
        for i in (2, 3, 4, 5):
            ya_sent[j, i].wait_recv()
        total = None
        for half in hs:
            for m in range(2):
                for q in range(4):
                    for cc in range(8):
                        to = cc * 64 + q * 16
                        rn[m, to : to + 16] = qg[n, q, m, half, cc // 2, (cc % 2) * 16 : (cc % 2) * 16 + 16]
            for m in range(2):
                lhs = strips[half, 4 * m : 4 * m + 4].reshape(512, 512)
                part = jnp.dot(lhs, rn[m], preferred_element_type=jnp.float32)
                total = part if total is None else (total + part if m == 0 else total - part)
        staged[n] = total if hs[0] == 0 else staged[n] + total
        if hs[-1] == 1:
            out = pltpu.make_async_copy(staged.at[n], out_ref.at[:, pl.ds(n * LN, LN)], out_sem.at[n])
            out.start()
            outs.append(out)

    steps = {"D": swap_density, "S0": strips_0, "S1": strips_1, "S2": strips_2, "S3": strips_3, "S4": strips_4}
    steps.update(a=a, r=r, b=b, c=c, e=e, g=g, h=h, k=k)
    for word in ORDER:
        name, _, j = word.partition(".")
        steps[name](int(j or 0))

    for cp in outs:
        cp.wait()
    for cp in started:
        cp.wait_send()

    @pl.when(p == 0)
    def _():
        for i in range(1, 8):
            copy(strip(i), strip(i), t0_ss.at[i], t0_rs, core_peer).wait_send()

    for o in range(1, 8):
        @pl.when(chip_of(o % 4 if o != 4 else 4) != 0)
        def _():
            copy(strip(p), strip(p), t_ss.at[o], t_rs.at[o], core_peer).wait_send()


def per_device(fock_matrix, intersection, density_panel, fock_mask, intersection_mask, density_mask):
    hbm = pl.BlockSpec(memory_space=pltpu.HBM)
    dma = pltpu.SemaphoreType.DMA
    bf16, f32, i16 = jnp.bfloat16, jnp.float32, jnp.int16
    return pl.pallas_call(
        kernel,
        out_shape=jax.ShapeDtypeStruct((512, 512), jnp.float32),
        in_specs=[hbm] * 6,
        out_specs=pl.BlockSpec(memory_space=pl.ANY),
        scratch_shapes=[
            pltpu.VMEM((512, 512), bf16),
            pltpu.VMEM((512, 512), bf16),
            pltpu.VMEM((4, 16, 512), bf16),
            pltpu.SMEM((1, 1), jnp.int32),
            pltpu.SMEM((1, 1), jnp.int32),
            pltpu.SMEM((1, 2), jnp.int32),
            dma((6,)),
            pltpu.VMEM((NC, 512, LN), f32),
            dma((NC,)),
            pltpu.VMEM((NC, 512, 2 * LN), bf16),
            pltpu.VMEM((4, 8, 2, 16, 512), bf16),
            pltpu.VMEM((NJ, 6, 2 * HR + SR, LN), i16),
            pltpu.VMEM((NJ, 6, 2 * HR + SR, LN), i16),
            pltpu.VMEM((NJ, 2, 2 * HR, LN), f32),
            pltpu.VMEM((NJ, 4, 4 * HZ + SR, LN), i16),
            pltpu.VMEM((NJ, 4, 4 * HZ + SR, LN), i16),
            pltpu.VMEM((NJ, 2, 2, 4, HZ, LN), f32),
            pltpu.VMEM((NC, 4, 2, 2, 4, HZ, LN), bf16),
            pltpu.VMEM((2, 8, 128, 512), bf16),
            pltpu.VMEM((2, 512, LN), bf16),
            dma((2, 8)), dma((2, 8)), dma((3,)), dma((3,)), dma((8,)), dma((8,)), dma((8,)), dma(()),
            dma((NJ, 6)), dma((NJ, 6)), dma((NJ, 4)), dma((NJ, 4)), dma((NJ, 4)), dma((NJ, 4)),
            dma((NJ, 6)), dma((NJ, 6)),
        ],
        compiler_params=pltpu.CompilerParams(
            collective_id=0, has_side_effects=True, vmem_limit_bytes=56 * 2**20
        ),
        cost_estimate=pl.CostEstimate(flops=2 * 2**30, bytes_accessed=3 * 2**20, transcendentals=0),
    )(
        fock_matrix,
        intersection,
        density_panel.reshape(4, 16, 512),
        fock_mask,
        intersection_mask,
        density_mask.T,
    )


def solution(mesh):
    placed = (
        P("row", "col"),
        P("row", "col"),
        P("col", "row"),
        P("row", "col"),
        P("row", "col"),
        P(None, "row"),
    )
    return jax.shard_map(
        per_device, mesh=mesh, in_specs=placed, out_specs=P("row", "col"), check_vma=False
    )
```

```python
import jax
import jax.numpy as jnp
from jax import lax
from jax.experimental import pallas as pl
from jax.experimental.pallas import tpu as pltpu
from jax.sharding import PartitionSpec as P

MESH = pl.DeviceIdType.MESH
NC = 4
LN = 128
SR = 16
HR = 128
HZ = 32
TOP = 32000.0
TINY = 2.0**-100
JOBS = ((0, (0, 1)), (1, (0, 1)), (2, (0, 1)), (3, (0,)), (3, (1,)))
NJ = len(JOBS)
ORDER = (
    "S0", "D.0", "a.0", "a.1", "D.1", "r.0", "r.1", "b.0", "a.2", "b.1", "r.2", "c.0", "a.3", "a.4",
    "b.2", "r.3", "r.4", "c.1", "b.3", "e.0", "b.4", "S1", "c.2", "e.1", "c.3", "g.0", "S2", "c.4",
    "e.2", "h.0", "g.1", "e.3", "e.4", "h.1", "g.2", "S3", "h.2", "g.3", "g.4", "S4", "k.0", "k.1",
    "h.3", "h.4", "k.2", "k.3", "k.4",
)


def encode(value):
    amax = jnp.max(jnp.abs(value), axis=0, keepdims=True)
    t = jnp.ceil(jnp.log2(jnp.maximum(amax, TINY)))
    q = jnp.round(value * (jnp.exp2(-t) * TOP)).astype(jnp.int32).astype(jnp.int16)
    return q, t


def decode(q, t):
    return q.astype(jnp.int32).astype(jnp.float32) * (jnp.exp2(t) * (1.0 / TOP))


def kernel(
    f_hbm, s_hbm, d_hbm, fm_hbm, sm_hbm, dm_hbm, out_ref,
    f_ref, s_ref, d_ref, fm_ref, sm_ref, dm_ref, in_sem, staged, out_sem,
    w, dg, ys, yr, pf, zs, zr, yq, qg, strips, rn,
    d_ss, d_rs, c_ss, c_rs, t_ss, t_rs, t0_ss, t0_rs,
    ys_ss, ys_rs, zs_ss, zs_rs, za_ss, za_rs, ya_ss, ya_rs,
):
    row, col = lax.axis_index("row"), lax.axis_index("col")
    y, zh = row // 4, row % 4
    zl, x, core = col // 8, (col // 2) % 4, col % 2
    p = zl * 4 + x

    def group_peer(o):
        return (row, ((zl + o // 4) % 2) * 8 + ((x + o % 4) % 4) * 2 + core)

    def chip_of(o):
        return ((zl + o // 4) % 2) * 4 + (x + o % 4) % 4

    def y_peer(d):
        return (((y + d) % 4) * 4 + zh, col)

    def z_peer(d):
        return (y * 4 + (zh + d) % 4, col)

    core_peer = (row, zl * 8 + x * 2 + 1 - core)
    up, down = y_peer(1), y_peer(3)

    started = []

    def copy(src, dst, ss, rs, to):
        return pltpu.make_async_remote_copy(
            src_ref=src, dst_ref=dst, send_sem=ss, recv_sem=rs, device_id=to, device_id_type=MESH
        )

    def send(src, dst, ss, rs, to):
        c = copy(src, dst, ss, rs, to)
        c.start()
        started.append(c)
        return c

    barrier = pltpu.get_barrier_semaphore()
    partners = [z_peer(d) for d in (2, 1, 3)] + [group_peer(o) for o in range(1, 8)]
    partners += [core_peer, up, down]
    for to in partners:
        pl.semaphore_signal(barrier, inc=1, device_id=to, device_id_type=MESH)

    ins = [
        pltpu.make_async_copy(src, dst, in_sem.at[i])
        for i, (src, dst) in enumerate(
            ((d_hbm, d_ref), (dm_hbm, dm_ref), (fm_hbm, fm_ref), (sm_hbm, sm_ref), (f_hbm, f_ref), (s_hbm, s_ref))
        )
    ]
    for cp in ins:
        cp.start()
    for cp in ins[:2]:
        cp.wait()
    dmask = dm_ref[0, zl].astype(jnp.float32)
    for d in range(4):
        rows = d_ref[(y + 2 + d) % 4]
        dg[d, p, core] = (rows.astype(jnp.float32) * dmask).astype(jnp.bfloat16)
    pl.semaphore_wait(barrier, len(partners))

    head, tail = pl.ds(0, 1), pl.ds(1, 3)
    d_sent = [
        [
            send(dg.at[part, p, core], dg.at[part, p, core], d_ss.at[i, o], d_rs.at[i, o], group_peer(o))
            for o in range(1, 8)
        ]
        for i, part in enumerate((head, tail))
    ]

    for cp in ins[2:]:
        cp.wait()
    fmask = fm_ref[0, 0].astype(jnp.float32)
    smask = sm_ref[0, 0].astype(jnp.float32)
    s_all = (s_ref[...].astype(jnp.float32) * smask).astype(jnp.bfloat16)
    f_all = (f_ref[...].astype(jnp.float32) * fmask).astype(jnp.bfloat16)
    for n in range(NC):
        w[n, :, :LN] = s_all[:, n * LN : (n + 1) * LN]
        w[n, :, LN:] = f_all[:, n * LN : (n + 1) * LN]

    @pl.when(p == 0)
    def _():
        for i in range(4):
            strips[core, i] = f_all[i * 128 : (i + 1) * 128]
            strips[core, 4 + i] = s_all[i * 128 : (i + 1) * 128]

    def swap_density(i):
        part = (head, tail)[i]
        for cp in d_sent[i]:
            cp.wait_recv()
        cp = send(dg.at[part, :, core], dg.at[part, :, core], c_ss.at[i], c_rs.at[i], core_peer)
        cp.wait_recv()

    def strip(i):
        return strips.at[core, i]

    def strips_0(_):
        @pl.when(p == 0)
        def _():
            for i in range(1, 8):
                copy(strip(i), strip(i), t0_ss.at[i], t0_rs, (row, 2 * i + core)).start()

    def strips_1(_):
        @pl.when(p != 0)
        def _():
            copy(strip(p), strip(p), t0_ss.at[0], t0_rs, core_peer).wait_recv()

        for o in (4, 2, 1, 3):
            @pl.when(chip_of(o) != 0)
            def _():
                copy(strip(p), strip(p), t_ss.at[o], t_rs.at[o], group_peer(o)).start()

    other = (1 - zl) * 4 + x

    def strips_2(_):
        @pl.when(p != 0)
        def _():
            copy(strip(other), strip(other), t_ss.at[4], t_rs.at[4], core_peer).wait_recv()

        for o in (2, 1, 3):
            @pl.when(chip_of(o) != 0)
            def _():
                copy(strip(other), strip(other), t_ss.at[4 + o], t_rs.at[4 + o], group_peer(o)).start()

    swaps = []
    outs = []

    def strips_3(_):
        @pl.when(p != 0)
        def _():
            for o in (1, 2, 3, 5, 6, 7):
                copy(strip(p), strip(p), t_ss.at[o], t_rs.at[o], core_peer).wait_recv()

        swaps.append(send(strips.at[core], strips.at[core], c_ss.at[2], c_rs.at[2], core_peer))

    def strips_4(_):
        swaps[0].wait_recv()

    def product(d, j):
        n, hs = JOBS[j]
        rows = dg[d, 4 * hs[0] : 4 * hs[-1] + 4].reshape(HR * len(hs), 512)
        return jnp.dot(rows, w[n], preferred_element_type=jnp.float32)

    y_sent = {}

    def send_y(j, i, value):
        q, t = encode(value)
        m = value.shape[0]
        ys[j, i, :m] = q
        ys[j, i, m : m + SR] = jnp.broadcast_to(t, (SR, LN)).astype(jnp.int32).astype(jnp.int16)
        part = pl.ds(0, m + SR)
        y_sent[j, i] = send(
            ys.at[j, i, part], yr.at[j, i, part], ys_ss.at[j, i], ys_rs.at[j, i], down if i % 2 else up
        )

    def recv_y(j, i):
        m = HR * len(JOBS[j][1])
        y_sent[j, i].wait_recv()
        t = yr[j, i, m : m + SR].astype(jnp.int32).astype(jnp.float32)[:1]
        return decode(yr[j, i, :m], t)

    def a(j):
        v = product(0, j)
        send_y(j, 0, v[:, :LN])
        send_y(j, 1, v[:, LN:])

    def r(j):
        m = HR * len(JOBS[j][1])
        v = product(3, j)
        send_y(j, 2, v[:, LN:])
        pf[j, 0, :m] = v[:, :LN]
        v = product(1, j)
        send_y(j, 3, v[:, :LN])
        pf[j, 1, :m] = v[:, LN:]

    def b(j):
        m = HR * len(JOBS[j][1])
        send_y(j, 4, pf[j, 0, :m] + recv_y(j, 0))
        send_y(j, 5, pf[j, 1, :m] + recv_y(j, 1))

    z_sent = {}

    def c(j):
        nh = len(JOBS[j][1])
        v = product(2, j)
        left = v[:, LN:] + recv_y(j, 2)
        right = v[:, :LN] + recv_y(j, 3)
        right = right + recv_y(j, 4)
        left = left + recv_y(j, 5)
        yq[j, 0, :nh] = right.reshape(nh, 4, HZ, LN)
        yq[j, 1, :nh] = left.reshape(nh, 4, HZ, LN)
        m = HZ * nh
        part = pl.ds(0, 2 * m + SR)
        for d in (2, 1, 3):
            to = (zh + d) % 4
            q0, t0 = encode(yq[j, 0, :nh, to].reshape(m, LN))
            q1, t1 = encode(yq[j, 1, :nh, to].reshape(m, LN))
            zs[j, d, :m] = q0
            zs[j, d, m : 2 * m] = q1
            t = jnp.concatenate([jnp.broadcast_to(t0, (8, LN)), jnp.broadcast_to(t1, (8, LN))], axis=0)
            zs[j, d, 2 * m : 2 * m + SR] = t.astype(jnp.int32).astype(jnp.int16)
            z_sent[j, d] = send(zs.at[j, d, part], zr.at[j, d, part], zs_ss.at[j, d], zs_rs.at[j, d], z_peer(d))

    za_sent = {}

    def e(j):
        n, hs = JOBS[j]
        nh = len(hs)
        m = HZ * nh
        right = yq[j, 0, :nh, zh].reshape(m, LN)
        left = yq[j, 1, :nh, zh].reshape(m, LN)
        for d in (1, 3, 2):
            z_sent[j, d].wait_recv()
            t = zr[j, d, 2 * m : 2 * m + SR].astype(jnp.int32).astype(jnp.float32)
            right = right + decode(zr[j, d, :m], t[:1])
            left = left + decode(zr[j, d, m : 2 * m], t[8:9])
        rows = slice(hs[0], hs[0] + nh)
        qg[n, y, 0, rows, zh] = right.astype(jnp.bfloat16).reshape(nh, HZ, LN)
        qg[n, y, 1, rows, zh] = left.astype(jnp.bfloat16).reshape(nh, HZ, LN)
        mine = qg.at[n, y, :, pl.ds(hs[0], nh), zh]
        for d in (2, 1, 3):
            za_sent[j, d] = send(mine, mine, za_ss.at[j, d], za_rs.at[j, d], z_peer(d))

    ya_sent = {}

    def g(j):
        n, hs = JOBS[j]
        for d in (1, 3, 2):
            za_sent[j, d].wait_recv()
        rows = pl.ds(hs[0], len(hs))
        for i, (m, to) in enumerate(((0, up), (1, down), (1, up), (0, down))):
            mine = qg.at[n, y, m, rows]
            ya_sent[j, i] = send(mine, mine, ya_ss.at[j, i], ya_rs.at[j, i], to)

    def h(j):
        n, hs = JOBS[j]
        rows = pl.ds(hs[0], len(hs))
        ya_sent[j, 0].wait_recv()
        part = qg.at[n, (y + 3) % 4, 0, rows]
        ya_sent[j, 4] = send(part, part, ya_ss.at[j, 4], ya_rs.at[j, 4], up)
        ya_sent[j, 1].wait_recv()
        part = qg.at[n, (y + 1) % 4, 1, rows]
        ya_sent[j, 5] = send(part, part, ya_ss.at[j, 5], ya_rs.at[j, 5], down)

    def k(j):
        n, hs = JOBS[j]
        for i in (2, 3, 4, 5):
            ya_sent[j, i].wait_recv()
        total = None
        for half in hs:
            for m in range(2):
                for q in range(4):
                    for cc in range(8):
                        to = cc * 64 + q * 16
                        rn[m, to : to + 16] = qg[n, q, m, half, cc // 2, (cc % 2) * 16 : (cc % 2) * 16 + 16]
            for m in range(2):
                lhs = strips[half, 4 * m : 4 * m + 4].reshape(512, 512)
                part = jnp.dot(lhs, rn[m], preferred_element_type=jnp.float32)
                total = part if total is None else (total + part if m == 0 else total - part)
        staged[n] = total if hs[0] == 0 else staged[n] + total
        if hs[-1] == 1:
            out = pltpu.make_async_copy(staged.at[n], out_ref.at[:, pl.ds(n * LN, LN)], out_sem.at[n])
            out.start()
            outs.append(out)

    steps = {"D": swap_density, "S0": strips_0, "S1": strips_1, "S2": strips_2, "S3": strips_3, "S4": strips_4}
    steps.update(a=a, r=r, b=b, c=c, e=e, g=g, h=h, k=k)
    for word in ORDER:
        name, _, j = word.partition(".")
        steps[name](int(j or 0))

    for cp in outs:
        cp.wait()
    for cp in started:
        cp.wait_send()

    @pl.when(p == 0)
    def _():
        for i in range(1, 8):
            copy(strip(i), strip(i), t0_ss.at[i], t0_rs, core_peer).wait_send()

    for o in range(1, 8):
        @pl.when(chip_of(o % 4 if o != 4 else 4) != 0)
        def _():
            copy(strip(p), strip(p), t_ss.at[o], t_rs.at[o], core_peer).wait_send()


def per_device(fock_matrix, intersection, density_panel, fock_mask, intersection_mask, density_mask):
    hbm = pl.BlockSpec(memory_space=pltpu.HBM)
    dma = pltpu.SemaphoreType.DMA
    bf16, f32, i16 = jnp.bfloat16, jnp.float32, jnp.int16
    return pl.pallas_call(
        kernel,
        out_shape=jax.ShapeDtypeStruct((512, 512), jnp.float32),
        in_specs=[hbm] * 6,
        out_specs=pl.BlockSpec(memory_space=pl.ANY),
        scratch_shapes=[
            pltpu.VMEM((512, 512), bf16),
            pltpu.VMEM((512, 512), bf16),
            pltpu.VMEM((4, 16, 512), bf16),
            pltpu.SMEM((1, 1), jnp.int32),
            pltpu.SMEM((1, 1), jnp.int32),
            pltpu.SMEM((1, 2), jnp.int32),
            dma((6,)),
            pltpu.VMEM((NC, 512, LN), f32),
            dma((NC,)),
            pltpu.VMEM((NC, 512, 2 * LN), bf16),
            pltpu.VMEM((4, 8, 2, 16, 512), bf16),
            pltpu.VMEM((NJ, 6, 2 * HR + SR, LN), i16),
            pltpu.VMEM((NJ, 6, 2 * HR + SR, LN), i16),
            pltpu.VMEM((NJ, 2, 2 * HR, LN), f32),
            pltpu.VMEM((NJ, 4, 4 * HZ + SR, LN), i16),
            pltpu.VMEM((NJ, 4, 4 * HZ + SR, LN), i16),
            pltpu.VMEM((NJ, 2, 2, 4, HZ, LN), f32),
            pltpu.VMEM((NC, 4, 2, 2, 4, HZ, LN), bf16),
            pltpu.VMEM((2, 8, 128, 512), bf16),
            pltpu.VMEM((2, 512, LN), bf16),
            dma((2, 8)), dma((2, 8)), dma((3,)), dma((3,)), dma((8,)), dma((8,)), dma((8,)), dma(()),
            dma((NJ, 6)), dma((NJ, 6)), dma((NJ, 4)), dma((NJ, 4)), dma((NJ, 4)), dma((NJ, 4)),
            dma((NJ, 6)), dma((NJ, 6)),
        ],
        compiler_params=pltpu.CompilerParams(
            collective_id=0, has_side_effects=True, vmem_limit_bytes=56 * 2**20
        ),
        cost_estimate=pl.CostEstimate(flops=2 * 2**30, bytes_accessed=3 * 2**20, transcendentals=0),
    )(
        fock_matrix,
        intersection,
        density_panel.reshape(4, 16, 512),
        fock_mask,
        intersection_mask,
        density_mask.T,
    )


def solution(mesh):
    placed = (
        P("row", "col"),
        P("row", "col"),
        P("col", "row"),
        P("row", "col"),
        P("row", "col"),
        P(None, "row"),
    )
    return jax.shard_map(
        per_device, mesh=mesh, in_specs=placed, out_specs=P("row", "col"), check_vma=False
    )
```
